32 devices in a mesh: groups: 2 (over y), tensor: 4 (over z), dp: 4 (over x, core).
Axes of the slice: x: 2, y: 2, z: 4, core: 2. Of those that a mesh axis runs over, the one named last changes fastest.
Arguments:
- gen_states: bfloat16 [64, 64, 8192], P(('groups', 'dp'), None, 'tensor'), parts along dimension 0, may hold values from -6 to 6
- lengths: int32 [64], P('groups'), parts along dimension 0, may hold values from 1 to 64
- route: int32 [64], P('groups'), parts along dimension 0, may hold values from 0 to 3, as said below
- ln_gain: float32 [8192], replicated, may hold values from 0.5 to 1.5
- w_query: bfloat16 [8192, 4096], P('dp', 'tensor'), may hold values from -1 to 1
- w_keyval: bfloat16 [4, 8192, 256], P(None, 'dp'), may hold values from -1 to 1
- w_out: bfloat16 [4096, 8192], P('tensor', 'dp'), may hold values from -0.125 to 0.125
- w_score: bfloat16 [3, 8192], P(None, 'tensor'), may hold values from -0.0625 to 0.0625
Outputs:
- reward_states: bfloat16 [64, 64, 8192], P(('groups', 'dp'), None, 'tensor'), parts along dimension 0
- scores: float32 [64, 3], P(('groups', 'dp')), parts along dimension 0
The draws below stay inside these ranges and needn't reach their ends.
There are 2 independent parts, one for each index of `groups`. The reference program is written for one: setup_inputs(seed, part) draws one part's arguments, and reference() takes and returns one part's arrays. A program takes and returns all parts, laid end to end along the dimension named above; an argument that names none is the same for every part. Nothing has to cross between parts.
Inputs may be any that keep to these rules, and one draw needn't show every extreme that they name: `route`: from each generator device (aligned blocks of 8 responses) exactly 2 responses go to each of 4 distinct reward devices, and every reward device receives exactly 8 responses.
All inputs are finite; a program needn't handle non-finite values.
Results may differ from the reference program's by a relative error of at most 0.0095.
The reference program's roundings to bfloat16 on the way count: a program that leaves them out, or rounds other values in their place, can miss the bound.
Values may be sent and summed in bfloat16 or wider, within the bound.
A program may use at most 192 MiB of HBM per device.

```python
import math
import jax
import jax.numpy as jnp
from jax import lax

D = 8192
HD = 128
QH = 32
KVH = 4
OBJ = 3
CAP = 2
RESP_DEV = 8
SLOT = 64
QPD = 8
RESP = 32
N_TENSOR = 4


def draw_lengths(key, part):
    key = jax.random.fold_in(key, 11)
    key_values, second = jax.random.split(key)
    drawn = jax.random.randint(key_values, (RESP,), 1, SLOT + 1)
    where_full = jax.random.randint(second, (), 0, RESP)
    return jnp.where(jnp.arange(RESP) == where_full, SLOT, drawn).astype(jnp.int32)


def draw_route(key, part):
    key = jax.random.fold_in(key, 23)
    devices = RESP // RESP_DEV
    key_target, key_shift, key_within = jax.random.split(key, 3)
    target = jax.random.permutation(key_target, devices)
    shifts = jax.random.permutation(key_shift, devices)[:RESP_DEV // CAP]
    within = jax.vmap(lambda sub_key: jax.random.permutation(sub_key, RESP_DEV))(jax.random.split(key_within, devices))
    source = jnp.arange(devices)[:, None]
    destination = target[(source + shifts[within // CAP]) % devices]
    return destination.reshape(RESP).astype(jnp.int32)


def draw_gen_states(key, part):
    key = jax.random.fold_in(key, 37)
    key_noise = jax.random.fold_in(key, 0)
    values = jnp.clip(jax.random.normal(key_noise, (RESP, SLOT, D), jnp.float32), -6.0, 6.0)
    return values.astype(jnp.bfloat16)


def draw_w_query(key, part):
    key = jax.random.fold_in(key, 41)
    values = jnp.clip(jax.random.normal(key, (D, QH * HD), jnp.float32), -6.0, 6.0) * D ** (-0.5)
    return jnp.clip(values, -1.0, 1.0).astype(jnp.bfloat16)


def draw_w_keyval(key, part):
    key = jax.random.fold_in(key, 53)
    values = jnp.clip(jax.random.normal(key, (KVH, D, 2 * HD), jnp.float32), -6.0, 6.0) * D ** (-0.5)
    return jnp.clip(values, -1.0, 1.0).astype(jnp.bfloat16)


def with_spikes(values, rng, source, target, parts, factor):
    def block_of(dim):
        return (jnp.arange(values.shape[dim]) // (values.shape[dim] // parts)).reshape((-1,) + (1,) * (values.ndim - 1 - dim))

    one_side = jax.random.permutation(rng, parts)[block_of(target)]
    far = (block_of(target) + parts // 2) % parts
    return jnp.where((block_of(source) == one_side) | (block_of(source) == far), factor * values, values)


def levels(rng, dims, shards, low, largest):
    def one(axis_at, blocks):
        heights = jax.random.uniform(jax.random.fold_in(jax.random.fold_in(rng, 6), axis_at), (blocks,), jnp.float32, low / len(shards), largest / len(shards))
        return jnp.repeat(jnp.exp(heights), dims[axis_at] // blocks).reshape((-1,) + (1,) * (len(dims) - axis_at - 1))

    gain = one(*shards[0])
    for cut in shards[1:]:
        gain = gain * one(*cut)
    return gain


def centred(rng, extent, spread, limit, pieces=(), held_as=jnp.bfloat16):
    loudness = levels(rng, extent, pieces, -0.22, 0.18) if pieces else 1.0
    values = jax.random.normal(rng, extent, jnp.float32) * spread * loudness
    return jnp.minimum(jnp.maximum(values, -limit), limit).astype(held_as)


def heavy_noise(rng, shape, deviation, reach, cuts, heavy, kind=jnp.bfloat16):
    values = deviation * jax.random.normal(rng, shape, jnp.float32)
    if cuts:
        values = values * levels(rng, shape, cuts, -0.22, 0.18)
    return jnp.clip(with_spikes(values, jax.random.fold_in(rng, 3), *heavy), -reach, reach).astype(kind)


def setup_inputs(seed: int = 0, part: int = 0) -> dict:
    key_list = jax.random.split(jax.random.key(seed), 9)
    part_splits = jax.random.split(jax.random.fold_in(key_list[8], part), 9)
    return {
        "gen_states": draw_gen_states(jax.random.fold_in(jax.random.fold_in(key_list[8], part), 71), part),
        "lengths": draw_lengths(jax.random.fold_in(jax.random.fold_in(key_list[8], part), 71), part),
        "route": draw_route(jax.random.fold_in(jax.random.fold_in(key_list[8], part), 71), part),
        "ln_gain": jnp.clip(1.0 + 0.1 * jax.random.normal(key_list[3], (D,), jnp.float32), 0.5, 1.5),
        "w_query": draw_w_query(jax.random.fold_in(key_list[8], 71), part),
        "w_keyval": draw_w_keyval(jax.random.fold_in(key_list[8], 71), part),
        "w_out": heavy_noise(key_list[6], (QH * HD, D), (QH * HD) ** -0.5, 0.125, ((0, 4), (1, 4)), (0, 1, 4, 2.0)),
        "w_score": centred(key_list[7], (OBJ, D), D ** -0.5, 0.0625, ((1, 4),)),
    }


EPS = 1e-05
THETA = 500000.0

def rotary_tables(row_count, period, head_size):
    positions = (jnp.arange(row_count, dtype=jnp.int32) % period).astype(jnp.float32)
    half_size = head_size // 2
    exponents = jnp.arange(half_size, dtype=jnp.float32) * (2.0 / head_size)
    inverse = jnp.power(jnp.float32(THETA), -exponents)
    angles = positions[:, None] * inverse[None, :]
    return (jnp.cos(angles), jnp.sin(angles))

def rotate(entries, cosine_table, sine_table):
    half_size = entries.shape[-1] // 2
    leading = entries[..., :half_size]
    back_part = entries[..., half_size:]
    return jnp.concatenate([leading * cosine_table - back_part * sine_table, back_part * cosine_table + leading * sine_table], axis=-1)

def reference(gen_states, lengths, route, ln_gain, w_query, w_keyval, w_out, w_score):
    reward_order = jnp.argsort(route, stable=True).astype(jnp.int32)
    states = jnp.take(gen_states, reward_order, axis=0)
    reward_lengths = jnp.take(lengths, reward_order, axis=0)
    row_total = RESP * SLOT
    flat_rows = states.reshape(row_total, D).astype(jnp.float32)
    mean_square = lax.optimization_barrier(jnp.mean(flat_rows * flat_rows, axis=1, keepdims=True))
    normed = (flat_rows * lax.rsqrt(mean_square + EPS) * ln_gain[None, :]).astype(jnp.bfloat16)
    cosine_table, sine_table = rotary_tables(row_total, SLOT, HD)
    queries = jnp.dot(normed, w_query, preferred_element_type=jnp.float32).reshape(row_total, QH, HD)
    queries = rotate(queries, cosine_table[:, None, :], sine_table[:, None, :]).astype(jnp.bfloat16)
    keys_list = []
    values_list = []
    for kv_head in range(KVH):
        keyval = jnp.dot(normed, w_keyval[kv_head], preferred_element_type=jnp.float32)
        keys_list.append(rotate(keyval[:, :HD], cosine_table, sine_table).astype(jnp.bfloat16))
        values_list.append(keyval[:, HD:].astype(jnp.bfloat16))
    share_count = QH // KVH
    keys_all = jnp.repeat(jnp.stack(keys_list, axis=1), share_count, axis=1)
    values_all = jnp.repeat(jnp.stack(values_list, axis=1), share_count, axis=1)
    causal = jnp.arange(SLOT)[:, None] >= jnp.arange(SLOT)[None, :]
    score_scale = 1.0 / math.sqrt(HD)

    def attend(block_in):
        query_block, key_block, value_block = block_in
        scores = jnp.einsum('qhd,khd->hqk', query_block.astype(jnp.float32), key_block.astype(jnp.float32)) * score_scale
        scores = jnp.where(causal[None], scores, -1e+30)
        row_peak = lax.optimization_barrier(jnp.max(scores, axis=2, keepdims=True))
        weights = jnp.exp(scores - row_peak)
        weights = (weights / lax.optimization_barrier(jnp.sum(weights, axis=2, keepdims=True))).astype(jnp.bfloat16)
        mixture = jnp.einsum('hqk,khd->qhd', weights.astype(jnp.float32), value_block.astype(jnp.float32))
        return mixture.astype(jnp.bfloat16)
    attended = lax.map(attend, (queries.reshape(RESP, SLOT, QH, HD), keys_all.reshape(RESP, SLOT, QH, HD), values_all.reshape(RESP, SLOT, QH, HD)))
    attended = attended.reshape(row_total, QH * HD)
    group_width = QPD * HD
    running = jnp.zeros((row_total, D), jnp.float32)
    for group_index in range(N_TENSOR):
        lower = group_index * group_width
        partial_value = jnp.dot(attended[:, lower:lower + group_width], w_out[lower:lower + group_width], preferred_element_type=jnp.float32)
        rounded = lax.optimization_barrier(partial_value.astype(jnp.bfloat16))
        running = running + rounded.astype(jnp.float32)
    positions = jnp.arange(row_total, dtype=jnp.int32) % SLOT
    validity = (positions < jnp.repeat(reward_lengths, SLOT)).astype(jnp.float32)
    reward_flat = ((flat_rows + running) * validity[:, None]).astype(jnp.bfloat16)
    reward_states = reward_flat.reshape(RESP, SLOT, D)
    last_index = jnp.arange(RESP, dtype=jnp.int32) * SLOT + reward_lengths - 1
    last_rows = jnp.take(reward_flat, last_index, axis=0)
    last_float = last_rows.astype(jnp.float32)
    last_square = lax.optimization_barrier(jnp.mean(last_float * last_float, axis=1, keepdims=True))
    head_dots = jnp.dot(last_rows, w_score.T, preferred_element_type=jnp.float32)
    reward_scores = head_dots * lax.rsqrt(last_square + EPS)
    scores = jnp.zeros((RESP, OBJ), jnp.float32).at[reward_order].set(reward_scores)
    return (reward_states, scores)
```

```python
import functools
import math

import jax
import jax.numpy as jnp
from jax import lax
from jax.experimental import pallas as pl
from jax.experimental.pallas import tpu as pltpu
from jax.sharding import PartitionSpec as P

D = 8192
HD = 128
QH = 32
KVH = 4
OBJ = 3
CAP = 2
CHUNKS = 2

EPS = 1e-05
THETA = 500000.0


def rotary_tables(row_count, period, head_size):
    positions = (jnp.arange(row_count, dtype=jnp.int32) % period).astype(jnp.float32)
    half_size = head_size // 2
    exponents = jnp.arange(half_size, dtype=jnp.float32) * (2.0 / head_size)
    inverse = jnp.power(jnp.float32(THETA), -exponents)
    angles = positions[:, None] * inverse[None, :]
    return (jnp.cos(angles), jnp.sin(angles))


def attention_kernel(heads, slot_len, q_ref, kv_ref, cos_ref, sin_ref, out_ref):
    rows = q_ref.shape[0]
    cosine, sine = cos_ref[...], sin_ref[...]

    def turn(x):
        return (x * cosine + pltpu.roll(x, HD // 2, 1) * sine).astype(jnp.bfloat16)

    key = turn(kv_ref[:, :HD])
    value = kv_ref[:, HD:].astype(jnp.bfloat16)
    row_ids = lax.broadcasted_iota(jnp.int32, (rows, rows), 0)
    key_ids = lax.broadcasted_iota(jnp.int32, (rows, rows), 1)
    allowed = (row_ids >= key_ids) & (row_ids // slot_len == key_ids // slot_len)
    for head in range(heads):
        query = turn(q_ref[:, head * HD:(head + 1) * HD])
        scores = lax.dot_general(
            query, key, (((1,), (1,)), ((), ())), preferred_element_type=jnp.float32
        ) * (1.0 / math.sqrt(HD))
        scores = jnp.where(allowed, scores, -1e30)
        weights = jnp.exp(scores - jnp.max(scores, axis=1, keepdims=True))
        weights = (weights / jnp.sum(weights, axis=1, keepdims=True)).astype(jnp.bfloat16)
        mixed = jnp.dot(weights, value, preferred_element_type=jnp.float32)
        out_ref[:, head * HD:(head + 1) * HD] = mixed.astype(jnp.bfloat16)


def attention(queries, keyval, cosine, sine, slot_len):
    row_count, width = queries.shape
    step = 2 * slot_len
    row_block = lambda i: (i, 0)
    return pl.pallas_call(
        functools.partial(attention_kernel, width // HD, slot_len),
        grid=(row_count // step,),
        in_specs=[
            pl.BlockSpec((step, width), row_block),
            pl.BlockSpec((step, 2 * HD), row_block),
            pl.BlockSpec((step, HD), lambda i: (0, 0)),
            pl.BlockSpec((step, HD), lambda i: (0, 0)),
        ],
        out_specs=pl.BlockSpec((step, width), row_block),
        out_shape=jax.ShapeDtypeStruct((row_count, width), jnp.bfloat16),
        cost_estimate=pl.CostEstimate(
            flops=row_count * step * width * 4,
            bytes_accessed=row_count * width * 6,
            transcendentals=row_count * step * width // HD,
        ),
    )(queries, keyval, cosine, sine)


def gather_dp(shard, axis):
    n = lax.axis_size("dp")
    groups = lax.axis_size("groups")
    me, group = lax.axis_index("dp"), lax.axis_index("groups")
    extent = shard.shape[axis]
    part = extent // groups
    shape = list(shard.shape)
    shape[axis] = n * extent
    full = jnp.zeros(shape, shard.dtype)

    def put(full, piece, start):
        where = [0] * len(shape)
        where[axis] = start
        return lax.dynamic_update_slice(full, piece, where)

    swap = [(i, i ^ 1) for i in range(n)]
    mine = lax.dynamic_slice_in_dim(shard, group * part, part, axis)
    pieces = []
    for chip in range(1, n // 2):
        far = lax.ppermute(mine, "dp", [(i, (i + 2 * chip) % n) for i in range(n)])
        source = (me - 2 * chip + n) % n
        pieces.append((far, source, group))
        for other in range(1, groups):
            passed = lax.ppermute(
                far, "groups", [(g, (g + other) % groups) for g in range(groups)]
            )
            pieces.append((passed, source, (group - other + groups) % groups))
    full = put(full, shard, me * extent)
    full = put(full, lax.ppermute(shard, "dp", swap), (me ^ 1) * extent)
    for piece, source, which in pieces:
        full = put(full, piece, source * extent + which * part)
        full = put(
            full, lax.ppermute(piece, "dp", swap), (source ^ 1) * extent + which * part
        )
    return full


def gather_line(block):
    count = lax.axis_size("tensor")
    up = [(i, i + 1) for i in range(count - 1)]
    down = [(i + 1, i) for i in range(count - 1)]
    rising, falling = [block], [block]
    for _ in range(count - 1):
        rising.append(lax.ppermute(rising[-1], "tensor", up))
        falling.append(lax.ppermute(falling[-1], "tensor", down))
    mine = lax.axis_index("tensor")
    return [block] + [
        jnp.where(mine >= s, rising[s], falling[count - s]) for s in range(1, count)
    ]


def sum_line(partial):
    count = lax.axis_size("tensor")
    mine = lax.axis_index("tensor")
    width = partial.shape[1] // count
    up = [(i, i + 1) for i in range(count - 1)]
    down = [(i + 1, i) for i in range(count - 1)]

    def block(index):
        index = jnp.clip(index, 0, count - 1)
        return lax.dynamic_slice_in_dim(partial, index * width, width, 1)

    rising = falling = None
    for step in range(count - 1):
        upward = block(mine + (count - 1 - step))
        downward = block(mine - (count - 1 - step))
        if step:
            upward = (upward.astype(jnp.float32) + rising.astype(jnp.float32)).astype(jnp.bfloat16)
            downward = (downward.astype(jnp.float32) + falling.astype(jnp.float32)).astype(jnp.bfloat16)
        rising = lax.ppermute(upward, "tensor", up)
        falling = lax.ppermute(downward, "tensor", down)
    return (
        block(mine).astype(jnp.float32)
        + rising.astype(jnp.float32)
        + falling.astype(jnp.float32)
    )


def body(gen_states, lengths, route, ln_gain, w_query, w_keyval, w_out, w_score):
    n = lax.axis_size("dp")
    me = lax.axis_index("dp")
    tensor_count = lax.axis_size("tensor")
    tensor_index = lax.axis_index("tensor")
    resp_dev, slot_len, width_part = gen_states.shape
    heads_here = w_query.shape[1] // HD
    row_count = resp_dev * slot_len
    route_table = route.reshape(n, resp_dev)
    my_routes = lax.dynamic_index_in_dim(route_table, me, 0, keepdims=False)
    slot_ids = jnp.arange(resp_dev, dtype=jnp.int32)
    earlier = slot_ids[None, :] < slot_ids[:, None]
    same_target = my_routes[:, None] == my_routes[None, :]
    sender_ranks = jnp.sum((earlier & same_target).astype(jnp.int32), axis=1)
    device_ids = jnp.arange(n, dtype=jnp.int32)
    capacity_ids = jnp.arange(CAP, dtype=jnp.int32)
    select = (my_routes[None, None, :] == device_ids[:, None, None]) & (
        sender_ranks[None, None, :] == capacity_ids[None, :, None]
    )
    picks = jnp.sum(jnp.where(select, slot_ids[None, None, :], 0), axis=2)
    arrivals = route_table == me
    counts = jnp.sum(arrivals.astype(jnp.int32), axis=1)
    offsets = jnp.cumsum(counts) - counts
    states = jnp.zeros((resp_dev + CAP, slot_len, width_part), gen_states.dtype)
    for shift in range(n):
        target = (me + shift) % n
        pair = jnp.concatenate(
            [
                lax.dynamic_slice_in_dim(gen_states, picks[target, j], 1, 0)
                for j in range(CAP)
            ],
            axis=0,
        )
        if shift:
            pair = lax.ppermute(pair, "dp", [(i, (i + shift) % n) for i in range(n)])
        source = (me - shift + n) % n
        start = jnp.where(counts[source] > 0, offsets[source], resp_dev)
        states = lax.dynamic_update_slice_in_dim(states, pair, start, 0)

    reward_ids = slot_ids
    placing = (
        reward_ids[:, None, None] == offsets[None, :, None] + capacity_ids[None, None, :]
    ) & (capacity_ids[None, None, :] < counts[None, :, None])
    placing = placing.reshape(resp_dev, n * CAP)
    flat_arrivals = arrivals.reshape(-1).astype(jnp.int32)
    places = jnp.cumsum(flat_arrivals) - 1
    owners = (places[None, :] == reward_ids[:, None]) & (flat_arrivals[None, :] == 1)
    reward_lengths = jnp.sum(jnp.where(owners, lengths[None, :], 0), axis=1)

    kv_index = tensor_index * heads_here // (QH // KVH)
    kv_shard = lax.dynamic_index_in_dim(w_keyval, kv_index, 0, keepdims=False)
    kv_full = gather_dp(kv_shard, 0)
    query_full = gather_dp(w_query, 0)
    out_full = gather_dp(w_out, 1)

    cosine, sine = rotary_tables(2 * slot_len, slot_len, HD)
    cosine = jnp.concatenate([cosine, cosine], axis=1)
    sine = jnp.concatenate([-sine, sine], axis=1)

    resp_chunk = resp_dev // CHUNKS
    rows_chunk = resp_chunk * slot_len
    outputs = []
    for chunk in range(CHUNKS):
        low = chunk * resp_chunk
        local = states[low:low + resp_chunk].reshape(rows_chunk, width_part)
        blocks = gather_line(local)
        full = jnp.zeros((rows_chunk, tensor_count * width_part), local.dtype)
        for s, piece in enumerate(blocks):
            owner = (tensor_index - s + tensor_count) % tensor_count
            full = lax.dynamic_update_slice_in_dim(full, piece, owner * width_part, 1)
        wide = full.astype(jnp.float32)
        mean_square = jnp.mean(wide * wide, axis=1, keepdims=True)
        normed = (wide * lax.rsqrt(mean_square + EPS) * ln_gain[None, :]).astype(jnp.bfloat16)
        queries = jnp.dot(normed, query_full, preferred_element_type=jnp.float32)
        keyval = jnp.dot(normed, kv_full, preferred_element_type=jnp.float32)
        attended = attention(queries, keyval, cosine, sine, slot_len)
        partial = jnp.dot(attended, out_full, preferred_element_type=jnp.float32)
        summed = sum_line(partial.astype(jnp.bfloat16))
        positions = jnp.arange(rows_chunk, dtype=jnp.int32) % slot_len
        valid = positions < jnp.repeat(reward_lengths[low:low + resp_chunk], slot_len)
        outputs.append(
            (
                (local.astype(jnp.float32) + summed) * valid.astype(jnp.float32)[:, None]
            ).astype(jnp.bfloat16)
        )
    reward_flat = jnp.concatenate(outputs, axis=0)

    last_index = reward_ids * slot_len + reward_lengths - 1
    last_rows = jnp.take(reward_flat, last_index, axis=0)
    last_float = last_rows.astype(jnp.float32)
    local_dots = jnp.dot(last_rows, w_score.T, preferred_element_type=jnp.float32)
    local_squares = jnp.sum(last_float * last_float, axis=1, keepdims=True)
    head_dots, square_sum = lax.psum((local_dots, local_squares), "tensor")
    reward_scores = head_dots * lax.rsqrt(square_sum / D + EPS)
    returning = jnp.dot(
        placing.T.astype(jnp.float32), reward_scores, precision=lax.Precision.HIGHEST
    ).reshape(n, CAP, OBJ)
    homecoming = lax.all_to_all(returning, "dp", split_axis=0, concat_axis=0, tiled=True)
    scores = jnp.dot(
        select.reshape(n * CAP, resp_dev).T.astype(jnp.float32),
        homecoming.reshape(n * CAP, OBJ),
        precision=lax.Precision.HIGHEST,
    )
    return (reward_flat.reshape(resp_dev, slot_len, width_part), scores)


def solution(mesh):
    in_specs = (
        P(("groups", "dp"), None, "tensor"),
        P("groups"),
        P("groups"),
        P(),
        P("dp", "tensor"),
        P(None, "dp", None),
        P("tensor", "dp"),
        P(None, "tensor"),
    )
    out_specs = (P(("groups", "dp"), None, "tensor"), P(("groups", "dp"), None))
    return jax.shard_map(body, mesh=mesh, in_specs=in_specs, out_specs=out_specs, check_vma=False)
```

```python
import functools
import math

import jax
import jax.numpy as jnp
from jax import lax
from jax.experimental import pallas as pl
from jax.experimental.pallas import tpu as pltpu
from jax.sharding import PartitionSpec as P

D = 8192
HD = 128
QH = 32
KVH = 4
OBJ = 3
CAP = 2
CHUNKS = 4
WPIECES = 4

EPS = 1e-05
THETA = 500000.0


def rotary_tables(row_count, period, head_size):
    positions = (jnp.arange(row_count, dtype=jnp.int32) % period).astype(jnp.float32)
    half_size = head_size // 2
    exponents = jnp.arange(half_size, dtype=jnp.float32) * (2.0 / head_size)
    inverse = jnp.power(jnp.float32(THETA), -exponents)
    angles = positions[:, None] * inverse[None, :]
    return (jnp.cos(angles), jnp.sin(angles))


MESH = pl.DeviceIdType.MESH


def kernel(dims, rows_ref, wq_hbm, kv_hbm, wo_hbm, gain_ref, cos_ref, sin_ref, out_hbm,
           wq, kv, wo, xg, up_slot, down_slot, queries, keyval, attended,
           own_sem, core_send, core_recv, x_send, x_recv, y_send, y_recv,
           own_core_send, own_core_recv,
           gather_send, gather_recv, sum_send, sum_recv, out_sem):
    n, groups, count, slot_len = dims
    chips = n // 2
    me, group, t = lax.axis_index("dp"), lax.axis_index("groups"), lax.axis_index("tensor")
    chunk_rows = xg.shape[2]
    chunks = xg.shape[0]
    width = xg.shape[3]
    heads = queries.shape[1] // HD
    mate = {"dp": me + 1 - 2 * lax.rem(me, 2)}
    above, below = {"tensor": t + 1}, {"tensor": t - 1}

    def remote(src, dst, send, recv, where):
        return pltpu.make_async_remote_copy(
            src_ref=src, dst_ref=dst, send_sem=send, recv_sem=recv,
            device_id=where, device_id_type=MESH)

    barrier = pltpu.get_barrier_semaphore()
    pl.semaphore_signal(barrier, inc=1, device_id=mate, device_id_type=MESH)
    for k in range(1, chips):
        pl.semaphore_signal(barrier, inc=1, device_id={"dp": lax.rem(me + 2 * k, n)}, device_id_type=MESH)
    for k in range(1, groups):
        pl.semaphore_signal(barrier, inc=1, device_id={"groups": lax.rem(group + k, groups)}, device_id_type=MESH)

    @pl.when(t < count - 1)
    def _():
        pl.semaphore_signal(barrier, inc=1, device_id=above, device_id_type=MESH)

    @pl.when(t > 0)
    def _():
        pl.semaphore_signal(barrier, inc=1, device_id=below, device_id_type=MESH)

    neighbours = jnp.where(t < count - 1, 1, 0) + jnp.where(t > 0, 1, 0)
    pl.semaphore_wait(barrier, 1 + (chips - 1) + (groups - 1) + neighbours)

    arrays = [(kv_hbm, kv, 1), (wq_hbm, wq, WPIECES), (wo_hbm, wo, WPIECES)]
    pieces = []
    for a, (shard, full, parts) in enumerate(arrays):
        size = shard.shape[0] // groups // parts
        for p in range(parts):
            pieces.append((a, shard, full, p, size))

    def place(i, device, which):
        a, shard, full, p, size = pieces[i]
        start = which * (shard.shape[0] // groups) + p * size
        return full.at[device, pl.ds(pl.multiple_of(start, size), size)]

    def x_copy(i, k):
        a, shard, full, p, size = pieces[i]
        start = group * (shard.shape[0] // groups) + p * size
        return remote(shard.at[pl.ds(pl.multiple_of(start, size), size)], place(i, me, group),
                      x_send.at[i, k - 1], x_recv.at[i, k - 1], {"dp": lax.rem(me + 2 * k, n)})

    def origin(k):
        return lax.rem(me - 2 * k + n, n)

    def y_copy(i, k, o):
        spot = place(i, origin(k), group)
        return remote(spot, spot, y_send.at[i, k - 1, o - 1], y_recv.at[i, k - 1, o - 1],
                      {"groups": lax.rem(group + o, groups)})

    def core_copy(i, k, o):
        spot = place(i, origin(k), lax.rem(group - o + groups, groups))
        return remote(spot, spot, core_send.at[i, k - 1, o], core_recv.at[i, k - 1, o], mate)

    def x_start(i):
        if i < len(pieces):
            for k in range(1, chips):
                x_copy(i, k).start()

    def x_event(i):
        for k in range(1, chips):
            x_copy(i, k).wait()
            for o in range(1, groups):
                y_copy(i, k, o).start()
            core_copy(i, k, 0).start()
        x_start(i + 2)

    def y_event(i):
        for k in range(1, chips):
            for o in range(1, groups):
                y_copy(i, k, o).wait()
                core_copy(i, k, o).start()

    def c_event(i):
        for k in range(1, chips):
            for o in range(groups):
                core_copy(i, k, o).wait()

    def own_copy(a):
        shard, full, _ = arrays[a]
        return pltpu.make_async_copy(shard, full.at[me], own_sem.at[a])

    def own_core(a):
        shard, full, _ = arrays[a]
        return remote(shard, full.at[me], own_core_send.at[a], own_core_recv.at[a], mate)

    def gather_copy(c, s, upward):
        d = 0 if upward else 1
        block = t - (s - 1) if upward else t + (s - 1)
        spot = xg.at[c, jnp.clip(block, 0, count - 1)]
        src = rows_ref.at[pl.ds(c * chunk_rows, chunk_rows)] if s == 1 else spot
        return remote(src, spot, gather_send.at[c, s - 1, d], gather_recv.at[c, s - 1, d],
                      above if upward else below)

    def gather_step(c, s):
        if c >= chunks:
            return
        for upward in (True, False):
            have = (t - (s - 1) >= 0) if upward else (t + (s - 1) <= count - 1)
            more = (t < count - 1) if upward else (t > 0)
            if s > 1:
                @pl.when(have)
                def _():
                    gather_copy(c, s - 1, upward).wait_recv()
            if s < count:
                @pl.when(have & more)
                def _():
                    gather_copy(c, s, upward).start()

    def gather_sent(c):
        for s in range(1, count):
            for upward in (True, False):
                have = (t - (s - 1) >= 0) if upward else (t + (s - 1) <= count - 1)
                more = (t < count - 1) if upward else (t > 0)

                @pl.when(have & more)
                def _():
                    gather_copy(c, s, upward).wait_send()

    def sum_copy(c, s, upward, edge):
        d = 0 if upward else 1
        slot = up_slot if upward else down_slot
        if edge:
            target = count - 1 - s if upward else s
            src = xg.at[c, target]
        else:
            src = slot.at[c, s - 1]
        return remote(src, slot.at[c, s], sum_send.at[c, s, d], sum_recv.at[c, s, d],
                      above if upward else below)

    def sum_step(c, s):
        for upward in (True, False):
            place_of = t if upward else count - 1 - t
            slot = up_slot if upward else down_slot

            @pl.when(place_of == 0)
            def _():
                sum_copy(c, s, upward, True).start()

            if s > 0:
                @pl.when((place_of > 0) & (place_of <= s))
                def _():
                    sum_copy(c, s - 1, upward, False if s > 1 else True).wait_recv()
                    target = count - 1 - s + t if upward else s - (count - 1 - t)
                    target = jnp.clip(target, 0, count - 1)

                    @pl.loop(0, chunk_rows // 16)
                    def _(r):
                        at = pl.ds(pl.multiple_of(r * 16, 16), 16)
                        slot[c, s - 1, at, :] = (
                            slot[c, s - 1, at, :].astype(jnp.float32)
                            + xg[c, target, at, :].astype(jnp.float32)
                        ).astype(jnp.bfloat16)

                    sum_copy(c, s, upward, False).start()

    def sum_end(c):
        last = count - 2

        @pl.when(t > 0)
        def _():
            sum_copy(c, last, True, True).wait_recv()

        @pl.when(t < count - 1)
        def _():
            sum_copy(c, last, False, True).wait_recv()

        def finish(terms):
            @pl.loop(0, chunk_rows // 16)
            def _(r):
                at = pl.ds(pl.multiple_of(r * 16, 16), 16)
                total = xg[c, t, at, :].astype(jnp.float32)
                for slot in terms:
                    total = total + slot[c, last, at, :].astype(jnp.float32)
                local = rows_ref[pl.ds(pl.multiple_of(c * chunk_rows + r * 16, 16), 16), :]
                xg[c, t, at, :] = (local.astype(jnp.float32) + total).astype(jnp.bfloat16)

        @pl.when(t == 0)
        def _():
            finish((down_slot,))

        @pl.when(t == count - 1)
        def _():
            finish((up_slot,))

        @pl.when((t > 0) & (t < count - 1))
        def _():
            finish((up_slot, down_slot))

        out_copy(c).start()

    def out_copy(c):
        return pltpu.make_async_copy(
            xg.at[c, t], out_hbm.at[pl.ds(c * chunk_rows, chunk_rows)], out_sem.at[c])

    def sum_sent(c):
        for s in range(count - 1):
            for upward in (True, False):
                place_of = t if upward else count - 1 - t

                @pl.when(place_of <= s)
                def _():
                    sum_copy(c, s, upward, True).wait_send()

    def norm(c):
        gather_sent(c)

        @pl.loop(0, chunk_rows // 16)
        def _(r):
            at = pl.ds(pl.multiple_of(r * 16, 16), 16)
            xg[c, t, at, :] = rows_ref[pl.ds(pl.multiple_of(c * chunk_rows + r * 16, 16), 16), :]
            total = jnp.zeros((16, 1), jnp.float32)
            for b in range(count):
                wide = xg[c, b, at, :].astype(jnp.float32)
                total = total + jnp.sum(wide * wide, axis=1, keepdims=True)
            scale = lax.rsqrt(total / (count * width) + EPS)
            for b in range(count):
                wide = xg[c, b, at, :].astype(jnp.float32)
                xg[c, b, at, :] = (wide * scale * gain_ref[:, b * width:(b + 1) * width]).astype(jnp.bfloat16)

    def project(c, full, target, tile):
        depth = full.shape[1]
        reach = min(depth, width)

        @pl.loop(0, target.shape[1] // tile)
        def _(i):
            cols = pl.ds(pl.multiple_of(i * tile, tile), tile)
            total = jnp.zeros((chunk_rows, tile), jnp.float32)
            for b in range(count * width // reach):
                d, inner = divmod(b * reach, depth)
                e, outer = divmod(b * reach, width)
                total = total + jnp.dot(
                    xg[c, e, :, outer:outer + reach],
                    full[d, inner:inner + reach, cols],
                    preferred_element_type=jnp.float32)
            target[:, cols] = total

    def attend():
        step = 2 * slot_len
        cosine, sine = cos_ref[...], sin_ref[...]

        def turn(x):
            return (x * cosine + pltpu.roll(x, HD // 2, 1) * sine).astype(jnp.bfloat16)

        row_ids = lax.broadcasted_iota(jnp.int32, (step, step), 0)
        key_ids = lax.broadcasted_iota(jnp.int32, (step, step), 1)
        first = row_ids < slot_len
        allowed = (row_ids >= key_ids) & ((key_ids >= slot_len) | first)
        for p in range(chunk_rows // step):
            at = slice(p * step, (p + 1) * step)
            key = turn(keyval[at, :HD])
            value = keyval[at, HD:].astype(jnp.bfloat16)
            for head in range(heads):
                here = slice(head * HD, (head + 1) * HD)
                scores = lax.dot_general(
                    turn(queries[at, here]), key, (((1,), (1,)), ((), ())),
                    preferred_element_type=jnp.float32) * (1.0 / math.sqrt(HD))
                scores = jnp.where(allowed, scores, -1e30)
                weights = jnp.exp(scores - jnp.max(scores, axis=1, keepdims=True))
                weights = (weights / jnp.sum(weights, axis=1, keepdims=True)).astype(jnp.bfloat16)
                attended[at, here] = jnp.dot(
                    weights, value, preferred_element_type=jnp.float32).astype(jnp.bfloat16)

    def output(c):
        span = wo.shape[2]
        tile = min(256, width)
        for j in range(count):
            d, base = divmod(j * width, span)

            @pl.loop(0, width // tile)
            def _(i):
                cols = pl.ds(pl.multiple_of(i * tile, tile), tile)
                wide = pl.ds(pl.multiple_of(base + i * tile, tile), tile)
                xg[c, j, :, cols] = jnp.dot(
                    attended[...], wo[d, :, wide],
                    preferred_element_type=jnp.float32).astype(jnp.bfloat16)

    total = len(pieces)
    early = 1 + WPIECES
    x_start(0)
    x_start(1)
    gather_step(0, 1)
    for a in range(3):
        own_core(a).start()
        own_copy(a).start()
    order = []
    for i in range(early):
        order.append((x_event, i))
        if i:
            order.append((y_event, i - 1))
    order.append((x_event, early))
    order.append((y_event, early - 1))
    steps = [(0, s) for s in range(2, count + 1)] + [(1, s) for s in range(1, count + 1)] + [(2, 1)]
    for i in range(max(len(order), len(steps))):
        if i < len(steps):
            gather_step(*steps[i])
        if i < len(order):
            order[i][0](order[i][1])
    for a in range(3):
        own_core(a).wait()
        own_copy(a).wait()
    for i in range(early):
        c_event(i)

    for c in range(chunks):
        if c == 0:
            x_event(early + 1)
            y_event(early)
        norm(c)
        project(c, kv, keyval, 256)
        if c:
            for s in range(1, count - 1):
                if s <= (count - 1) // 2:
                    sum_step(c - 1, s)
        project(c, wq, queries, 256)
        for s in range(2, count // 2 + 1):
            gather_step(c + 2, s)
        if c:
            for s in range(1, count - 1):
                if s > (count - 1) // 2:
                    sum_step(c - 1, s)
        attend()
        for s in range(count // 2 + 1, count):
            gather_step(c + 2, s)
        if c == 0:
            for i in range(early + 1, total):
                if i + 1 < total:
                    x_event(i + 1)
                y_event(i)
            for i in range(early, total):
                c_event(i)
        output(c)
        sum_step(c, 0)
        if c:
            sum_end(c - 1)
        gather_step(c + 2, count)
        gather_step(c + 3, 1)
    for s in range(1, count - 1):
        sum_step(chunks - 1, s)
    sum_end(chunks - 1)
    for c in range(chunks):
        sum_sent(c)
        out_copy(c).wait()


def layer(local, w_query, kv_shard, w_out, ln_gain, cosine, sine, slot_len):
    n, groups, count = lax.axis_size("dp"), lax.axis_size("groups"), lax.axis_size("tensor")
    rows, width = local.shape
    chunk_rows = rows // CHUNKS
    pieces = 1 + 2 * WPIECES
    dma = pltpu.SemaphoreType.DMA
    chips = n // 2
    hops = max(1, chips - 1)
    others = max(1, groups - 1)
    whole = pl.BlockSpec(memory_space=pltpu.VMEM)
    remain = pl.BlockSpec(memory_space=pl.ANY)
    heads_width = w_query.shape[1]
    bf16 = jnp.bfloat16
    return pl.pallas_call(
        functools.partial(kernel, (n, groups, count, slot_len)),
        out_shape=jax.ShapeDtypeStruct((rows, width), bf16),
        in_specs=[whole, remain, remain, remain, whole, whole, whole],
        out_specs=remain,
        scratch_shapes=[
            pltpu.VMEM((n,) + w_query.shape, bf16),
            pltpu.VMEM((n,) + kv_shard.shape, bf16),
            pltpu.VMEM((n,) + w_out.shape, bf16),
            pltpu.VMEM((CHUNKS, count, chunk_rows, width), bf16),
            pltpu.VMEM((CHUNKS, count - 1, chunk_rows, width), bf16),
            pltpu.VMEM((CHUNKS, count - 1, chunk_rows, width), bf16),
            pltpu.VMEM((chunk_rows, heads_width), jnp.float32),
            pltpu.VMEM((chunk_rows, 2 * HD), jnp.float32),
            pltpu.VMEM((chunk_rows, heads_width), bf16),
            dma((3,)),
            dma((pieces, hops, groups)), dma((pieces, hops, groups)),
            dma((pieces, hops)), dma((pieces, hops)),
            dma((pieces, hops, others)), dma((pieces, hops, others)),
            dma((3,)), dma((3,)),
            dma((CHUNKS, count, 2)), dma((CHUNKS, count, 2)),
            dma((CHUNKS, count, 2)), dma((CHUNKS, count, 2)),
            dma((CHUNKS,)),
        ],
        compiler_params=pltpu.CompilerParams(
            collective_id=0, has_side_effects=True, vmem_limit_bytes=63 * 1024 * 1024),
        cost_estimate=pl.CostEstimate(
            flops=rows * D * heads_width * 5, bytes_accessed=60 * 2**20, transcendentals=rows * 2**10),
    )(local, w_query, kv_shard, w_out, ln_gain.reshape(1, -1), cosine, sine)


def body(gen_states, lengths, route, ln_gain, w_query, w_keyval, w_out, w_score):
    n = lax.axis_size("dp")
    me = lax.axis_index("dp")
    tensor_count = lax.axis_size("tensor")
    tensor_index = lax.axis_index("tensor")
    resp_dev, slot_len, width_part = gen_states.shape
    heads_here = w_query.shape[1] // HD
    row_count = resp_dev * slot_len
    route_table = route.reshape(n, resp_dev)
    my_routes = lax.dynamic_index_in_dim(route_table, me, 0, keepdims=False)
    slot_ids = jnp.arange(resp_dev, dtype=jnp.int32)
    earlier = slot_ids[None, :] < slot_ids[:, None]
    same_target = my_routes[:, None] == my_routes[None, :]
    sender_ranks = jnp.sum((earlier & same_target).astype(jnp.int32), axis=1)
    device_ids = jnp.arange(n, dtype=jnp.int32)
    capacity_ids = jnp.arange(CAP, dtype=jnp.int32)
    select = (my_routes[None, None, :] == device_ids[:, None, None]) & (
        sender_ranks[None, None, :] == capacity_ids[None, :, None]
    )
    picks = jnp.sum(jnp.where(select, slot_ids[None, None, :], 0), axis=2)
    arrivals = route_table == me
    counts = jnp.sum(arrivals.astype(jnp.int32), axis=1)
    offsets = jnp.cumsum(counts) - counts
    states = jnp.zeros((resp_dev + CAP, slot_len, width_part), gen_states.dtype)
    for shift in range(n):
        target = (me + shift) % n
        pair = jnp.concatenate(
            [
                lax.dynamic_slice_in_dim(gen_states, picks[target, j], 1, 0)
                for j in range(CAP)
            ],
            axis=0,
        )
        if shift:
            pair = lax.ppermute(pair, "dp", [(i, (i + shift) % n) for i in range(n)])
        source = (me - shift + n) % n
        start = jnp.where(counts[source] > 0, offsets[source], resp_dev)
        states = lax.dynamic_update_slice_in_dim(states, pair, start, 0)

    reward_ids = slot_ids
    placing = (
        reward_ids[:, None, None] == offsets[None, :, None] + capacity_ids[None, None, :]
    ) & (capacity_ids[None, None, :] < counts[None, :, None])
    placing = placing.reshape(resp_dev, n * CAP)
    flat_arrivals = arrivals.reshape(-1).astype(jnp.int32)
    places = jnp.cumsum(flat_arrivals) - 1
    owners = (places[None, :] == reward_ids[:, None]) & (flat_arrivals[None, :] == 1)
    reward_lengths = jnp.sum(jnp.where(owners, lengths[None, :], 0), axis=1)

    kv_index = tensor_index * heads_here // (QH // KVH)
    kv_shard = lax.dynamic_index_in_dim(w_keyval, kv_index, 0, keepdims=False)
    cosine, sine = rotary_tables(2 * slot_len, slot_len, HD)
    cosine = jnp.concatenate([cosine, cosine], axis=1)
    sine = jnp.concatenate([-sine, sine], axis=1)

    local = states[:resp_dev].reshape(row_count, width_part)
    summed = layer(local, w_query, kv_shard, w_out, ln_gain, cosine, sine, slot_len)
    positions = jnp.arange(row_count, dtype=jnp.int32) % slot_len
    valid = positions < jnp.repeat(reward_lengths, slot_len)
    reward_flat = jnp.where(valid[:, None], summed, 0).astype(jnp.bfloat16)

    last_index = reward_ids * slot_len + reward_lengths - 1
    last_rows = jnp.take(reward_flat, last_index, axis=0)
    last_float = last_rows.astype(jnp.float32)
    local_dots = jnp.dot(last_rows, w_score.T, preferred_element_type=jnp.float32)
    local_squares = jnp.sum(last_float * last_float, axis=1, keepdims=True)
    head_dots, square_sum = lax.psum((local_dots, local_squares), "tensor")
    reward_scores = head_dots * lax.rsqrt(square_sum / D + EPS)
    returning = jnp.dot(
        placing.T.astype(jnp.float32), reward_scores, precision=lax.Precision.HIGHEST
    ).reshape(n, CAP, OBJ)
    homecoming = lax.all_to_all(returning, "dp", split_axis=0, concat_axis=0, tiled=True)
    scores = jnp.dot(
        select.reshape(n * CAP, resp_dev).T.astype(jnp.float32),
        homecoming.reshape(n * CAP, OBJ),
        precision=lax.Precision.HIGHEST,
    )
    return (reward_flat.reshape(resp_dev, slot_len, width_part), scores)


def solution(mesh):
    in_specs = (
        P(("groups", "dp"), None, "tensor"),
        P("groups"),
        P("groups"),
        P(),
        P("dp", "tensor"),
        P(None, "dp", None),
        P("tensor", "dp"),
        P(None, "tensor"),
    )
    out_specs = (P(("groups", "dp"), None, "tensor"), P(("groups", "dp"), None))
    return jax.shard_map(body, mesh=mesh, in_specs=in_specs, out_specs=out_specs, check_vma=False)
```

```python
import functools
import math

import jax
import jax.numpy as jnp
from jax import lax
from jax.experimental import pallas as pl
from jax.experimental.pallas import tpu as pltpu
from jax.sharding import PartitionSpec as P

D = 8192
HD = 128
QH = 32
KVH = 4
OBJ = 3
CAP = 2
CHUNKS = 4
WPIECES = 4

EPS = 1e-05
THETA = 500000.0


def rotary_tables(row_count, period, head_size):
    positions = (jnp.arange(row_count, dtype=jnp.int32) % period).astype(jnp.float32)
    half_size = head_size // 2
    exponents = jnp.arange(half_size, dtype=jnp.float32) * (2.0 / head_size)
    inverse = jnp.power(jnp.float32(THETA), -exponents)
    angles = positions[:, None] * inverse[None, :]
    return (jnp.cos(angles), jnp.sin(angles))


MESH = pl.DeviceIdType.MESH


def kernel(dims, rows_ref, wq_hbm, kv_hbm, wo_hbm, gain_ref, cos_ref, sin_ref, out_hbm,
           wq, kv, wo, xg, up_slot, down_slot, queries, keyval, attended,
           own_sem, core_send, core_recv, x_send, x_recv, y_send, y_recv,
           own_core_send, own_core_recv,
           gather_send, gather_recv, sum_send, sum_recv, out_sem):
    n, groups, count, slot_len = dims
    chips = n // 2
    me, group, t = lax.axis_index("dp"), lax.axis_index("groups"), lax.axis_index("tensor")
    chunk_rows = xg.shape[2]
    chunks = xg.shape[0]
    width = xg.shape[3]
    heads = queries.shape[1] // HD
    mate = {"dp": me + 1 - 2 * lax.rem(me, 2)}
    above, below = {"tensor": t + 1}, {"tensor": t - 1}

    def remote(src, dst, send, recv, where):
        return pltpu.make_async_remote_copy(
            src_ref=src, dst_ref=dst, send_sem=send, recv_sem=recv,
            device_id=where, device_id_type=MESH)

    barrier = pltpu.get_barrier_semaphore()
    pl.semaphore_signal(barrier, inc=1, device_id=mate, device_id_type=MESH)
    for k in range(1, chips):
        pl.semaphore_signal(barrier, inc=1, device_id={"dp": lax.rem(me + 2 * k, n)}, device_id_type=MESH)
    for k in range(1, groups):
        pl.semaphore_signal(barrier, inc=1, device_id={"groups": lax.rem(group + k, groups)}, device_id_type=MESH)

    @pl.when(t < count - 1)
    def _():
        pl.semaphore_signal(barrier, inc=1, device_id=above, device_id_type=MESH)

    @pl.when(t > 0)
    def _():
        pl.semaphore_signal(barrier, inc=1, device_id=below, device_id_type=MESH)

    neighbours = jnp.where(t < count - 1, 1, 0) + jnp.where(t > 0, 1, 0)
    pl.semaphore_wait(barrier, 1 + (chips - 1) + (groups - 1) + neighbours)

    arrays = [(kv_hbm, kv, 1), (wq_hbm, wq, WPIECES), (wo_hbm, wo, WPIECES)]
    pieces = []
    for a, (shard, full, parts) in enumerate(arrays):
        size = shard.shape[0] // groups // parts
        for p in range(parts):
            pieces.append((a, shard, full, p, size))

    def place(i, device, which):
        a, shard, full, p, size = pieces[i]
        start = which * (shard.shape[0] // groups) + p * size
        return full.at[device, pl.ds(pl.multiple_of(start, size), size)]

    def x_copy(i, k):
        a, shard, full, p, size = pieces[i]
        start = group * (shard.shape[0] // groups) + p * size
        return remote(shard.at[pl.ds(pl.multiple_of(start, size), size)], place(i, me, group),
                      x_send.at[i, k - 1], x_recv.at[i, k - 1], {"dp": lax.rem(me + 2 * k, n)})

    def origin(k):
        return lax.rem(me - 2 * k + n, n)

    def y_copy(i, k, o):
        spot = place(i, origin(k), group)
        return remote(spot, spot, y_send.at[i, k - 1, o - 1], y_recv.at[i, k - 1, o - 1],
                      {"groups": lax.rem(group + o, groups)})

    def core_copy(i, k, o):
        spot = place(i, origin(k), lax.rem(group - o + groups, groups))
        return remote(spot, spot, core_send.at[i, k - 1, o], core_recv.at[i, k - 1, o], mate)

    def x_start(i):
        if i < len(pieces):
            for k in range(1, chips):
                x_copy(i, k).start()

    def x_event(i):
        for k in range(1, chips):
            x_copy(i, k).wait()
            for o in range(1, groups):
                y_copy(i, k, o).start()
            core_copy(i, k, 0).start()
        x_start(i + 3)

    def y_event(i):
        for k in range(1, chips):
            for o in range(1, groups):
                y_copy(i, k, o).wait()
                core_copy(i, k, o).start()

    def c_event(i):
        for k in range(1, chips):
            for o in range(groups):
                core_copy(i, k, o).wait()

    def own_copy(a):
        shard, full, _ = arrays[a]
        return pltpu.make_async_copy(shard, full.at[me], own_sem.at[a])

    def own_core(a):
        shard, full, _ = arrays[a]
        return remote(shard, full.at[me], own_core_send.at[a], own_core_recv.at[a], mate)

    def gather_copy(c, s, upward):
        d = 0 if upward else 1
        block = t - (s - 1) if upward else t + (s - 1)
        spot = xg.at[c, jnp.clip(block, 0, count - 1)]
        src = rows_ref.at[pl.ds(c * chunk_rows, chunk_rows)] if s == 1 else spot
        return remote(src, spot, gather_send.at[c, s - 1, d], gather_recv.at[c, s - 1, d],
                      above if upward else below)

    def gather_step(c, s):
        if c >= chunks:
            return
        for upward in (True, False):
            have = (t - (s - 1) >= 0) if upward else (t + (s - 1) <= count - 1)
            more = (t < count - 1) if upward else (t > 0)
            if s > 1:
                @pl.when(have)
                def _():
                    gather_copy(c, s - 1, upward).wait_recv()
            if s < count:
                @pl.when(have & more)
                def _():
                    gather_copy(c, s, upward).start()

    def gather_sent(c):
        for s in range(1, count):
            for upward in (True, False):
                have = (t - (s - 1) >= 0) if upward else (t + (s - 1) <= count - 1)
                more = (t < count - 1) if upward else (t > 0)

                @pl.when(have & more)
                def _():
                    gather_copy(c, s, upward).wait_send()

    def sum_copy(c, s, upward, edge):
        d = 0 if upward else 1
        slot = up_slot if upward else down_slot
        if edge:
            target = count - 1 - s if upward else s
            src = xg.at[c, target]
        else:
            src = slot.at[c, s - 1]
        return remote(src, slot.at[c, s], sum_send.at[c, s, d], sum_recv.at[c, s, d],
                      above if upward else below)

    def sum_step(c, s):
        for upward in (True, False):
            place_of = t if upward else count - 1 - t
            slot = up_slot if upward else down_slot

            if s == 0:
                @pl.when(place_of == 0)
                def _():
                    for later in range(count - 1):
                        sum_copy(c, later, upward, True).start()

            if s > 0:
                @pl.when((place_of > 0) & (place_of <= s))
                def _():
                    sum_copy(c, s - 1, upward, False if s > 1 else True).wait_recv()
                    target = count - 1 - s + t if upward else s - (count - 1 - t)
                    target = jnp.clip(target, 0, count - 1)

                    @pl.loop(0, chunk_rows // 16)
                    def _(r):
                        at = pl.ds(pl.multiple_of(r * 16, 16), 16)
                        slot[c, s - 1, at, :] = (
                            slot[c, s - 1, at, :].astype(jnp.float32)
                            + xg[c, target, at, :].astype(jnp.float32)
                        ).astype(jnp.bfloat16)

                    sum_copy(c, s, upward, False).start()

    def sum_end(c):
        last = count - 2

        @pl.when(t > 0)
        def _():
            sum_copy(c, last, True, True).wait_recv()

        @pl.when(t < count - 1)
        def _():
            sum_copy(c, last, False, True).wait_recv()

        def finish(terms):
            @pl.loop(0, chunk_rows // 16)
            def _(r):
                at = pl.ds(pl.multiple_of(r * 16, 16), 16)
                total = xg[c, t, at, :].astype(jnp.float32)
                for slot in terms:
                    total = total + slot[c, last, at, :].astype(jnp.float32)
                local = rows_ref[pl.ds(pl.multiple_of(c * chunk_rows + r * 16, 16), 16), :]
                xg[c, t, at, :] = (local.astype(jnp.float32) + total).astype(jnp.bfloat16)

        @pl.when(t == 0)
        def _():
            finish((down_slot,))

        @pl.when(t == count - 1)
        def _():
            finish((up_slot,))

        @pl.when((t > 0) & (t < count - 1))
        def _():
            finish((up_slot, down_slot))

        out_copy(c).start()

    def out_copy(c):
        return pltpu.make_async_copy(
            xg.at[c, t], out_hbm.at[pl.ds(c * chunk_rows, chunk_rows)], out_sem.at[c])

    def sum_sent(c):
        for s in range(count - 1):
            for upward in (True, False):
                place_of = t if upward else count - 1 - t

                @pl.when(place_of <= s)
                def _():
                    sum_copy(c, s, upward, True).wait_send()

    def norm(c):
        gather_sent(c)

        @pl.loop(0, chunk_rows // 16)
        def _(r):
            at = pl.ds(pl.multiple_of(r * 16, 16), 16)
            xg[c, t, at, :] = rows_ref[pl.ds(pl.multiple_of(c * chunk_rows + r * 16, 16), 16), :]
            total = jnp.zeros((16, 1), jnp.float32)
            for b in range(count):
                wide = xg[c, b, at, :].astype(jnp.float32)
                total = total + jnp.sum(wide * wide, axis=1, keepdims=True)
            scale = lax.rsqrt(total / (count * width) + EPS)
            for b in range(count):
                wide = xg[c, b, at, :].astype(jnp.float32)
                xg[c, b, at, :] = (wide * scale * gain_ref[:, b * width:(b + 1) * width]).astype(jnp.bfloat16)

    def project(c, full, target, tile):
        depth = full.shape[1]
        reach = min(depth, width)

        @pl.loop(0, target.shape[1] // tile)
        def _(i):
            cols = pl.ds(pl.multiple_of(i * tile, tile), tile)
            total = jnp.zeros((chunk_rows, tile), jnp.float32)
            for b in range(count * width // reach):
                d, inner = divmod(b * reach, depth)
                e, outer = divmod(b * reach, width)
                total = total + jnp.dot(
                    xg[c, e, :, outer:outer + reach],
                    full[d, inner:inner + reach, cols],
                    preferred_element_type=jnp.float32)
            target[:, cols] = total

    def attend():
        step = 2 * slot_len
        cosine, sine = cos_ref[...], sin_ref[...]

        def turn(x):
            return (x * cosine + pltpu.roll(x, HD // 2, 1) * sine).astype(jnp.bfloat16)

        row_ids = lax.broadcasted_iota(jnp.int32, (step, step), 0)
        key_ids = lax.broadcasted_iota(jnp.int32, (step, step), 1)
        first = row_ids < slot_len
        allowed = (row_ids >= key_ids) & ((key_ids >= slot_len) | first)
        for p in range(chunk_rows // step):
            at = slice(p * step, (p + 1) * step)
            key = turn(keyval[at, :HD])
            value = keyval[at, HD:].astype(jnp.bfloat16)
            for head in range(heads):
                here = slice(head * HD, (head + 1) * HD)
                scores = lax.dot_general(
                    turn(queries[at, here]), key, (((1,), (1,)), ((), ())),
                    preferred_element_type=jnp.float32) * (1.0 / math.sqrt(HD))
                scores = jnp.where(allowed, scores, -1e30)
                weights = jnp.exp(scores - jnp.max(scores, axis=1, keepdims=True))
                weights = (weights / jnp.sum(weights, axis=1, keepdims=True)).astype(jnp.bfloat16)
                attended[at, here] = jnp.dot(
                    weights, value, preferred_element_type=jnp.float32).astype(jnp.bfloat16)

    def output(c):
        span = wo.shape[2]
        tile = min(256, width)
        for j in range(count):
            d, base = divmod(j * width, span)

            @pl.loop(0, width // tile)
            def _(i):
                cols = pl.ds(pl.multiple_of(i * tile, tile), tile)
                wide = pl.ds(pl.multiple_of(base + i * tile, tile), tile)
                xg[c, j, :, cols] = jnp.dot(
                    attended[...], wo[d, :, wide],
                    preferred_element_type=jnp.float32).astype(jnp.bfloat16)

    total = len(pieces)
    early = 1 + WPIECES
    x_start(0)
    x_start(1)
    x_start(2)
    gather_step(0, 1)
    for a in range(3):
        own_core(a).start()
        own_copy(a).start()
    order = []
    for i in range(early):
        order.append((x_event, i))
        if i:
            order.append((y_event, i - 1))
    order.append((x_event, early))
    order.append((y_event, early - 1))
    steps = [(0, s) for s in range(2, count + 1)] + [(1, s) for s in range(1, count + 1)] + [(2, 1)]
    for i in range(max(len(order), len(steps))):
        if i < len(steps):
            gather_step(*steps[i])
        if i < len(order):
            order[i][0](order[i][1])
    for a in range(3):
        own_core(a).wait()
        own_copy(a).wait()
    for i in range(early):
        c_event(i)

    for c in range(chunks):
        if c == 0:
            x_event(early + 1)
            y_event(early)
        norm(c)
        project(c, kv, keyval, 256)
        if c:
            for s in range(1, count - 1):
                if s <= (count - 1) // 2:
                    sum_step(c - 1, s)
        project(c, wq, queries, 256)
        if c == 0:
            hops = [(2, s) for s in range(2, count + 1)] + [(3, 1)]
            for i in range(early + 1, total):
                if i + 1 < total:
                    x_event(i + 1)
                if hops:
                    gather_step(*hops.pop(0))
                y_event(i)
            for hop in hops:
                gather_step(*hop)
            attend()
            for i in range(early, total):
                c_event(i)
        else:
            for s in range(2, count // 2 + 1):
                gather_step(c + 2, s)
            for s in range(1, count - 1):
                if s > (count - 1) // 2:
                    sum_step(c - 1, s)
            attend()
            for s in range(count // 2 + 1, count):
                gather_step(c + 2, s)
        output(c)
        sum_step(c, 0)
        if c:
            gather_step(c + 2, count)
            gather_step(c + 3, 1)
        if c > 1:
            sum_end(c - 2)
    for s in range(1, count - 1):
        sum_step(chunks - 1, s)
    for c in range(max(chunks - 2, 0), chunks):
        sum_end(c)
    for c in range(chunks):
        sum_sent(c)
        out_copy(c).wait()


def layer(local, w_query, kv_shard, w_out, ln_gain, cosine, sine, slot_len):
    n, groups, count = lax.axis_size("dp"), lax.axis_size("groups"), lax.axis_size("tensor")
    rows, width = local.shape
    chunk_rows = rows // CHUNKS
    pieces = 1 + 2 * WPIECES
    dma = pltpu.SemaphoreType.DMA
    chips = n // 2
    hops = max(1, chips - 1)
    others = max(1, groups - 1)
    whole = pl.BlockSpec(memory_space=pltpu.VMEM)
    remain = pl.BlockSpec(memory_space=pl.ANY)
    heads_width = w_query.shape[1]
    bf16 = jnp.bfloat16
    return pl.pallas_call(
        functools.partial(kernel, (n, groups, count, slot_len)),
        out_shape=jax.ShapeDtypeStruct((rows, width), bf16),
        in_specs=[whole, remain, remain, remain, whole, whole, whole],
        out_specs=remain,
        scratch_shapes=[
            pltpu.VMEM((n,) + w_query.shape, bf16),
            pltpu.VMEM((n,) + kv_shard.shape, bf16),
            pltpu.VMEM((n,) + w_out.shape, bf16),
            pltpu.VMEM((CHUNKS, count, chunk_rows, width), bf16),
            pltpu.VMEM((CHUNKS, count - 1, chunk_rows, width), bf16),
            pltpu.VMEM((CHUNKS, count - 1, chunk_rows, width), bf16),
            pltpu.VMEM((chunk_rows, heads_width), jnp.float32),
            pltpu.VMEM((chunk_rows, 2 * HD), jnp.float32),
            pltpu.VMEM((chunk_rows, heads_width), bf16),
            dma((3,)),
            dma((pieces, hops, groups)), dma((pieces, hops, groups)),
            dma((pieces, hops)), dma((pieces, hops)),
            dma((pieces, hops, others)), dma((pieces, hops, others)),
            dma((3,)), dma((3,)),
            dma((CHUNKS, count, 2)), dma((CHUNKS, count, 2)),
            dma((CHUNKS, count, 2)), dma((CHUNKS, count, 2)),
            dma((CHUNKS,)),
        ],
        compiler_params=pltpu.CompilerParams(
            collective_id=0, has_side_effects=True, vmem_limit_bytes=63 * 1024 * 1024),
        cost_estimate=pl.CostEstimate(
            flops=rows * D * heads_width * 5, bytes_accessed=60 * 2**20, transcendentals=rows * 2**10),
    )(local, w_query, kv_shard, w_out, ln_gain.reshape(1, -1), cosine, sine)


def body(gen_states, lengths, route, ln_gain, w_query, w_keyval, w_out, w_score):
    n = lax.axis_size("dp")
    me = lax.axis_index("dp")
    tensor_count = lax.axis_size("tensor")
    tensor_index = lax.axis_index("tensor")
    resp_dev, slot_len, width_part = gen_states.shape
    heads_here = w_query.shape[1] // HD
    row_count = resp_dev * slot_len
    route_table = route.reshape(n, resp_dev)
    my_routes = lax.dynamic_index_in_dim(route_table, me, 0, keepdims=False)
    slot_ids = jnp.arange(resp_dev, dtype=jnp.int32)
    earlier = slot_ids[None, :] < slot_ids[:, None]
    same_target = my_routes[:, None] == my_routes[None, :]
    sender_ranks = jnp.sum((earlier & same_target).astype(jnp.int32), axis=1)
    device_ids = jnp.arange(n, dtype=jnp.int32)
    capacity_ids = jnp.arange(CAP, dtype=jnp.int32)
    select = (my_routes[None, None, :] == device_ids[:, None, None]) & (
        sender_ranks[None, None, :] == capacity_ids[None, :, None]
    )
    picks = jnp.sum(jnp.where(select, slot_ids[None, None, :], 0), axis=2)
    arrivals = route_table == me
    counts = jnp.sum(arrivals.astype(jnp.int32), axis=1)
    offsets = jnp.cumsum(counts) - counts
    states = jnp.zeros((resp_dev + CAP, slot_len, width_part), gen_states.dtype)
    for shift in range(n):
        target = (me + shift) % n
        pair = jnp.concatenate(
            [
                lax.dynamic_slice_in_dim(gen_states, picks[target, j], 1, 0)
                for j in range(CAP)
            ],
            axis=0,
        )
        if shift:
            pair = lax.ppermute(pair, "dp", [(i, (i + shift) % n) for i in range(n)])
        source = (me - shift + n) % n
        start = jnp.where(counts[source] > 0, offsets[source], resp_dev)
        states = lax.dynamic_update_slice_in_dim(states, pair, start, 0)

    reward_ids = slot_ids
    placing = (
        reward_ids[:, None, None] == offsets[None, :, None] + capacity_ids[None, None, :]
    ) & (capacity_ids[None, None, :] < counts[None, :, None])
    placing = placing.reshape(resp_dev, n * CAP)
    flat_arrivals = arrivals.reshape(-1).astype(jnp.int32)
    places = jnp.cumsum(flat_arrivals) - 1
    owners = (places[None, :] == reward_ids[:, None]) & (flat_arrivals[None, :] == 1)
    reward_lengths = jnp.sum(jnp.where(owners, lengths[None, :], 0), axis=1)

    kv_index = tensor_index * heads_here // (QH // KVH)
    kv_shard = lax.dynamic_index_in_dim(w_keyval, kv_index, 0, keepdims=False)
    cosine, sine = rotary_tables(2 * slot_len, slot_len, HD)
    cosine = jnp.concatenate([cosine, cosine], axis=1)
    sine = jnp.concatenate([-sine, sine], axis=1)

    local = states[:resp_dev].reshape(row_count, width_part)
    summed = layer(local, w_query, kv_shard, w_out, ln_gain, cosine, sine, slot_len)
    positions = jnp.arange(row_count, dtype=jnp.int32) % slot_len
    valid = positions < jnp.repeat(reward_lengths, slot_len)
    reward_flat = jnp.where(valid[:, None], summed, 0).astype(jnp.bfloat16)

    last_index = reward_ids * slot_len + reward_lengths - 1
    last_rows = jnp.take(reward_flat, last_index, axis=0)
    last_float = last_rows.astype(jnp.float32)
    local_dots = jnp.dot(last_rows, w_score.T, preferred_element_type=jnp.float32)
    local_squares = jnp.sum(last_float * last_float, axis=1, keepdims=True)
    head_dots, square_sum = lax.psum((local_dots, local_squares), "tensor")
    reward_scores = head_dots * lax.rsqrt(square_sum / D + EPS)
    returning = jnp.dot(
        placing.T.astype(jnp.float32), reward_scores, precision=lax.Precision.HIGHEST
    ).reshape(n, CAP, OBJ)
    homecoming = lax.all_to_all(returning, "dp", split_axis=0, concat_axis=0, tiled=True)
    scores = jnp.dot(
        select.reshape(n * CAP, resp_dev).T.astype(jnp.float32),
        homecoming.reshape(n * CAP, OBJ),
        precision=lax.Precision.HIGHEST,
    )
    return (reward_flat.reshape(resp_dev, slot_len, width_part), scores)


def solution(mesh):
    in_specs = (
        P(("groups", "dp"), None, "tensor"),
        P("groups"),
        P("groups"),
        P(),
        P("dp", "tensor"),
        P(None, "dp", None),
        P("tensor", "dp"),
        P(None, "tensor"),
    )
    out_specs = (P(("groups", "dp"), None, "tensor"), P(("groups", "dp"), None))
    return jax.shard_map(body, mesh=mesh, in_specs=in_specs, out_specs=out_specs, check_vma=False)
```
